1024 devices in a mesh: row: 32 (over z, y_hi, core), col: 32 (over x, y_lo).
Axes of the slice: x: 8, y: 8 (y_hi: 2, y_lo: 4; y = y_hi * 4 + y_lo), z: 8, core: 2. Of those that a mesh axis runs over, the one named last changes fastest.
Arguments:
- matrix_blocks: bfloat16 [32, 128, 4096], P('row', 'col'), may hold values from -6 to 6
- block_codes: int32 [32, 128], P('row', 'col'), may hold values from 0 to 16383, as said below
- block_perm: int32 [128], replicated, may hold values from 0 to 127, as said below
- grid_blocks: bfloat16 [32, 2048, 4096], P('row', 'col'), may hold values from -2.4 to 2.4, as said below
- grid_tasks: int32 [32, 2048], P('row', 'col'), may hold values from -1 to 16383, as said below
Outputs:
- square: bfloat16 [32, 128, 4096], P('row', 'col')
- sign_next: bfloat16 [32, 128, 4096], P('row', 'col')
The draws below stay inside these ranges and needn't reach their ends.
Inputs may be any that keep to these rules, and one draw needn't show every extreme that they name: `block_perm`: A permutation of 0 to 127. `block_codes`: index (r, c) stores 4 different positions, each with block row in [r * 4, (r + 1) * 4) and block column in [c * 4, (c + 1) * 4). `grid_tasks`: index (r, c) holds 32 groups of 2 slots; a live item in group j names a position stored by index (r, j); in every index of row one owner receives 2 live items from every sender of its row. `grid_blocks`: empty slots hold zeros.
All inputs are finite; a program needn't handle non-finite values.
Results may differ from the reference program's by a relative error of at most 0.0058.
Values may be sent and summed in bfloat16 or wider, within the bound.
No kernel may reach another device: no remote copies, remote signals or barrier semaphores. Data moves between devices by JAX's collectives and lax.ppermute only.
A program may use at most 64 MiB of HBM per device.

```python
import math
import jax
import jax.numpy as jnp
from jax import lax

BS = 64
S = 4
CAP = 2
RT = 4
NBLK = 128
CT = 4
N_ROW = 32
N_COL = 32


def common_draw(key):
    key_perm = jax.random.fold_in(key, 11)
    key_slots = jax.random.fold_in(key, 12)
    key_counts = jax.random.fold_in(key, 13)
    key_busiest = jax.random.fold_in(key, 14)
    key_target = jax.random.fold_in(key, 15)
    position_of = jax.random.permutation(key_perm, NBLK).astype(jnp.int32)
    inverse = jnp.argsort(position_of).astype(jnp.int32)
    place_count = RT * CT
    target_pos = position_of[NBLK - 1]
    target_row = target_pos // RT
    target_col = target_pos // CT
    target_place = target_pos % RT * CT + target_pos % CT
    row_ids = jnp.arange(N_ROW, dtype=jnp.int32)[:, None, None]
    col_ids = jnp.arange(N_COL, dtype=jnp.int32)[None, :, None]
    place_ids = jnp.arange(place_count, dtype=jnp.int32)[None, None, :]
    forced = (row_ids == 0) & (col_ids == 0) & (place_ids == 0) | (row_ids == N_ROW - 1) & (col_ids == N_COL - 1) & (place_ids == place_count - 1) | (row_ids == target_row) & (col_ids == target_col) & (place_ids == target_place)
    scores = jax.random.randint(key_slots, (N_ROW, N_COL, place_count), 0, 1 << 20) * place_count + jnp.arange(place_count, dtype=jnp.int32)
    scores = jnp.where(forced, -1, scores)
    ordering = jnp.argsort(scores, axis=-1)[:, :, :S].astype(jnp.int32)
    row_pos = jnp.arange(N_ROW, dtype=jnp.int32)[:, None, None] * RT + ordering // CT
    col_pos = jnp.arange(N_COL, dtype=jnp.int32)[None, :, None] * CT + ordering % CT
    codes = (row_pos * NBLK + col_pos).astype(jnp.int32)
    counts = jax.random.randint(key_counts, (N_ROW, N_COL, N_COL), 0, CAP + 1)
    busiest = jax.random.randint(key_busiest, (N_ROW,), 0, N_COL)
    owner_axis = jnp.arange(N_COL, dtype=jnp.int32)[None, None, :]
    counts = jnp.where(owner_axis == busiest[:, None, None], CAP, counts)
    slot_ids = jnp.arange(CAP, dtype=jnp.int32)[None, None, None, :]
    is_live = slot_ids < counts[..., None]
    row_four = jnp.arange(N_ROW, dtype=jnp.int32)[:, None, None, None]
    sender_four = jnp.arange(N_COL, dtype=jnp.int32)[None, :, None, None]
    owner_four = jnp.arange(N_COL, dtype=jnp.int32)[None, None, :, None]
    special = (row_four == target_row) & (sender_four == 0) & (owner_four == target_col) & (slot_ids == 0)
    emptied = (row_four == 0) & (sender_four == N_COL - 1) & (owner_four == (busiest[0] + 1) % N_COL) & (slot_ids == CAP - 1)
    is_live = (is_live | special) & jnp.logical_not(emptied)
    target = jax.random.randint(key_target, (N_ROW, N_COL, N_COL, CAP), 0, S)
    owner_codes = jnp.broadcast_to(codes[:, None, :, :], (N_ROW, N_COL, N_COL, S))
    chosen = jnp.take_along_axis(owner_codes, target, axis=3)
    initial = inverse[chosen // NBLK] * NBLK + inverse[chosen % NBLK]
    initial = jnp.where(special, NBLK * NBLK - 1, initial)
    task_list = jnp.where(is_live, initial, -1).reshape(N_ROW, N_COL * N_COL * CAP).astype(jnp.int32)
    return (position_of, codes.reshape(N_ROW, N_COL * S), task_list, is_live.reshape(N_ROW, N_COL * N_COL * CAP))


def draw_block_perm(key, part):
    return common_draw(key)[0]


def draw_block_codes(key, part):
    return common_draw(key)[1]


def draw_grid_tasks(key, part):
    return common_draw(key)[2]


def draw_grid_blocks(key, part):
    is_live = common_draw(key)[3]
    key = jax.random.fold_in(key, 7)
    array_shape = (N_ROW, N_COL * N_COL * CAP, BS * BS)
    values = jnp.clip(0.4 * jax.random.normal(key, array_shape), -2.4, 2.4)
    return jnp.where(is_live[..., None], values, 0.0).astype(jnp.bfloat16)


def levels(own_key, shape, cuts, low, largest):
    level, own = 1.0, jax.random.fold_in(own_key, 6)
    for dim, shards_of in cuts:
        steps = jnp.exp(jax.random.uniform(jax.random.fold_in(own, dim), (shards_of,), jnp.float32, low / len(cuts), largest / len(cuts)))
        level = level * jnp.repeat(steps, shape[dim] // shards_of).reshape([-1 if axis == dim else 1 for axis in range(len(shape))])
    return level


def gaussian(rng, dims, width, reach, cuts=(), kind=jnp.bfloat16):
    entries = width * jax.random.normal(rng, dims, jnp.float32)
    if cuts:
        entries = entries * levels(rng, dims, cuts, -0.22, 0.18)
    return jnp.clip(entries, -reach, reach).astype(kind)


def setup_inputs(seed: int = 0) -> dict:
    key_of = jax.random.split(jax.random.key(seed), 6)
    matrix_blocks = gaussian(key_of[0], (N_ROW, N_COL * S, BS * BS), 1.0, 6.0, ((0, 32), (1, 32)))
    block_codes = draw_block_codes(jax.random.fold_in(key_of[5], 71), 0)
    block_perm = draw_block_perm(jax.random.fold_in(key_of[5], 71), 0)
    grid_blocks = draw_grid_blocks(jax.random.fold_in(key_of[5], 71), 0)
    grid_tasks = draw_grid_tasks(jax.random.fold_in(key_of[5], 71), 0)
    return dict(matrix_blocks=matrix_blocks, block_codes=block_codes, block_perm=block_perm, grid_blocks=grid_blocks, grid_tasks=grid_tasks)


def tile_terms(left_panel, left_codes_all, right_blocks, right_codes, own_codes, block_count, tile_cols):
    right_row = right_codes // block_count
    right_col = right_codes % block_count
    tile_index = right_row // tile_cols
    left_blocks = jnp.take(left_panel, tile_index, axis=0)
    left_codes = jnp.take(left_codes_all, tile_index, axis=0)
    left_row = left_codes // block_count
    left_col = left_codes % block_count
    own_row = own_codes // block_count
    own_col = own_codes % block_count
    selector = (left_row[None] == own_row[:, None, None]) & (left_col[None] == right_row[None, :, None]) & (right_col[None, :, None] == own_col[:, None, None])
    chosen = jnp.einsum('cba,baik->cbik', selector.astype(jnp.float32), left_blocks.astype(jnp.float32), precision=lax.Precision.HIGHEST)
    return jnp.einsum('cbik,bkj->cij', chosen, right_blocks.astype(jnp.float32), precision=lax.Precision.HIGHEST)

def filtered(left_all, right_all, codes):
    block_count = RT * N_ROW
    tile_cols = block_count // N_COL
    left_tiles = left_all.reshape(N_ROW, N_COL, S, BS, BS)
    right_tiles = right_all.reshape(N_ROW, N_COL, S, BS, BS)
    code_tiles = codes.reshape(N_ROW, N_COL, S)

    def one_device(device_index):
        row_index = device_index // N_COL
        col_index = device_index % N_COL
        left_panel = left_tiles[row_index]
        left_codes_all = code_tiles[row_index]
        right_blocks = jnp.take(right_tiles, col_index, axis=1).reshape(N_ROW * S, BS, BS)
        right_codes = jnp.take(code_tiles, col_index, axis=1).reshape(N_ROW * S)
        own_codes = code_tiles[row_index, col_index]
        return tile_terms(left_panel, left_codes_all, right_blocks, right_codes, own_codes, block_count, tile_cols)
    result = lax.map(one_device, jnp.arange(N_ROW * N_COL, dtype=jnp.int32))
    return result.reshape(N_ROW, N_COL * S, BS * BS)

def reference(matrix_blocks, block_codes, block_perm, grid_blocks, grid_tasks):
    block_count = RT * N_ROW

    def owner_row(row_index):
        task_list = grid_tasks[row_index]
        items = grid_blocks[row_index]
        own_codes = block_codes[row_index]
        is_live = task_list >= 0
        task_safe = jnp.where(is_live, task_list, 0)
        position = block_perm[task_safe // block_count] * block_count + block_perm[task_safe % block_count]
        matches = (position[:, None] == own_codes[None, :]) & is_live[:, None]
        return jnp.einsum('ms,mf->sf', matches.astype(jnp.float32), items.astype(jnp.float32), precision=lax.Precision.HIGHEST)
    grid_sum = lax.map(owner_row, jnp.arange(N_ROW, dtype=jnp.int32))
    matrix = (matrix_blocks.astype(jnp.float32) + grid_sum).astype(jnp.bfloat16)
    scale_factor = 1.5 / math.sqrt(BS * S * N_COL / RT)
    square = (scale_factor * filtered(matrix, matrix, block_codes)).astype(jnp.bfloat16)
    second = filtered(matrix, square, block_codes)
    sign_next = (1.5 * matrix.astype(jnp.float32) - 0.5 * scale_factor * second).astype(jnp.bfloat16)
    return (square, sign_next)
```

```python
import math

import jax
import jax.numpy as jnp
from jax import lax
from jax.experimental import pallas as pl
from jax.experimental.pallas import tpu as pltpu
from jax.sharding import PartitionSpec as P

BS = 64
SLOTS = 4
SIDE = 4
TILE = BS * SIDE
VMEM = pl.BlockSpec(memory_space=pltpu.VMEM)
SMEM = pl.BlockSpec(memory_space=pltpu.SMEM)


def lookup(indices, table):
    positions = jnp.arange(table.shape[0], dtype=jnp.int32)
    return jnp.sum(jnp.where(indices[:, None] == positions[None, :], table[None, :], 0), axis=1)


def pack(blocks):
    return blocks.reshape(2, 2, BS, BS).transpose(0, 2, 1, 3).reshape(2, BS, 2 * BS)


def unpack(pairs):
    return pairs.reshape(2, BS, 2, BS).transpose(0, 2, 1, 3).reshape(SLOTS, BS * BS)


def swap_halves(x):
    return jnp.concatenate([x[:, BS:], x[:, :BS]], axis=1)


def place(dense, row, column, pair, slot, where_, masks):
    half = where_ % 2
    moved = jnp.where(half == slot % 2, pair, swap_halves(pair))
    kept = moved * jnp.where(half == 0, masks[0], masks[1])
    rows = pl.ds(pl.multiple_of(row + (where_ // SIDE) * BS, BS), BS)
    columns = pl.ds(pl.multiple_of(column + ((where_ % SIDE) // 2) * 2 * BS, 2 * BS), 2 * BS)
    dense[rows, columns] = dense[rows, columns] + kept


def lane_masks():
    lane = lax.broadcasted_iota(jnp.int32, (BS, 2 * BS), 1)
    low = jnp.where(lane < BS, 1.0, 0.0).astype(jnp.bfloat16)
    return low, (1.0 - low.astype(jnp.float32)).astype(jnp.bfloat16)


def fill_left(dense, panel, codes):
    masks = lane_masks()
    dense[...] = jnp.zeros_like(dense)

    def body(t, carry):
        for slot in range(SLOTS):
            place(dense, 0, t * TILE, panel[t, slot // 2], slot, codes[t * SLOTS + slot], masks)
        return carry

    lax.fori_loop(0, panel.shape[0], body, 0)


def fill_right(dense, panels, codes, core):
    masks = lane_masks()
    dense[...] = jnp.zeros_like(dense)
    for which, panel in enumerate(panels):

        def body(a, carry, which=which, panel=panel):
            t = 2 * a + (core if which == 0 else 1 - core)
            for slot in range(SLOTS):
                pair = panel[a, pl.ds((slot // 2) * BS, BS), :]
                place(dense, t * TILE, 0, pair, slot, codes[t * SLOTS + slot], masks)
            return carry

        lax.fori_loop(0, panel.shape[0], body, 0)


def own_pairs(total, own):
    lane = lax.broadcasted_iota(jnp.int32, (BS, 2 * BS), 1)
    pairs = []
    for pair in range(2):
        parts = []
        for slot in (2 * pair, 2 * pair + 1):
            where_ = own[slot]
            rows = pl.ds(pl.multiple_of((where_ // SIDE) * BS, BS), BS)
            columns = pl.ds(pl.multiple_of(((where_ % SIDE) // 2) * 2 * BS, 2 * BS), 2 * BS)
            block = total[rows, columns]
            parts.append(jnp.where(where_ % 2 == slot % 2, block, pltpu.roll(block, BS, 1)))
        pairs.append(jnp.where(lane < BS, parts[0], parts[1]))
    return pairs


def first_kernel(
    scale, codes_left, codes_right, own, core, left, mine, other, square, dense_left, dense_right, total
):
    fill_right(dense_right, (mine, other), codes_right, core[0])
    fill_left(dense_left, left, codes_left)
    total[...] = jnp.dot(dense_left[...], dense_right[...], preferred_element_type=jnp.float32)
    for pair, value in enumerate(own_pairs(total, own)):
        square[pair] = (scale * value).astype(square.dtype)


def second_kernel(
    scale, codes_right, own, core, dense_left, mine, other, matrix, sign_next, dense_right, total
):
    fill_right(dense_right, (mine, other), codes_right, core[0])
    total[...] = jnp.dot(dense_left[...], dense_right[...], preferred_element_type=jnp.float32)
    for pair, value in enumerate(own_pairs(total, own)):
        before = matrix[pair].astype(jnp.float32)
        sign_next[pair] = (1.5 * before - 0.5 * scale * value).astype(sign_next.dtype)


def local(matrix_blocks, block_codes, block_perm, grid_blocks, grid_tasks):
    col_count = lax.axis_size("col")
    row_count = lax.axis_size("row")
    block_count = block_perm.shape[0]
    tile_rows = block_count // row_count
    tile_cols = block_count // col_count
    bf16 = jnp.bfloat16
    barrier = lax.optimization_barrier
    core = lax.axis_index("row") % 2
    own_codes = block_codes[0]
    own_place = (own_codes // block_count) % tile_rows * SIDE + own_codes % tile_cols

    tasks = grid_tasks[0]
    safe = jnp.maximum(tasks, 0)
    place_row = lookup(safe // block_count, block_perm) % tile_rows
    place_col = lookup(safe % block_count, block_perm) % tile_cols
    item_place = jnp.where(tasks >= 0, place_row * SIDE + place_col, -1)
    cap = tasks.shape[0] // col_count
    tail = jnp.concatenate(
        [
            item_place[:, None].astype(bf16),
            jnp.broadcast_to(own_place.astype(bf16)[None], (tasks.shape[0], SLOTS)),
            jnp.zeros((tasks.shape[0], 128 - 1 - SLOTS), bf16),
        ],
        axis=1,
    )
    payload = jnp.concatenate([grid_blocks[0], tail], axis=1).reshape(col_count, cap, -1)
    received = lax.all_to_all(payload, "col", 0, 0, tiled=True)
    codes_left = received[:, 0, BS * BS + 1 : BS * BS + 1 + SLOTS].astype(jnp.int32).reshape(-1)
    arrived_place = received[:, :, BS * BS].astype(jnp.int32).reshape(-1)
    items = received[:, :, : BS * BS].reshape(-1, BS * BS)
    matches = (own_place[:, None] == arrived_place[None, :]).astype(bf16)
    grid_sum = jnp.dot(matches, items, preferred_element_type=jnp.float32)
    matrix = (matrix_blocks[0].astype(jnp.float32) + grid_sum).astype(bf16)
    pairs = barrier(pack(matrix))

    runs = [[x * 4 + y for y in range(4)] for x in range(col_count // 4)]
    lines = [[x * 4 + y for x in range(col_count // 4)] for y in range(4)]
    near = lax.all_to_all(
        jnp.broadcast_to(pairs[None], (4,) + pairs.shape),
        "col", 0, 0, axis_index_groups=runs, tiled=True,
    )
    left = lax.all_to_all(
        jnp.broadcast_to(near[None], (col_count // 4,) + near.shape),
        "col", 0, 0, axis_index_groups=lines, tiled=True,
    ).reshape((col_count,) + pairs.shape)

    cores = [[2 * chip + one for chip in range(row_count // 2)] for one in range(2)]
    swap = [(i, i ^ 1) for i in range(row_count)]

    def column_panel(rows):
        chips = row_count // 2
        mine = lax.all_to_all(
            jnp.broadcast_to(rows[None], (chips,) + rows.shape),
            "row", 0, 0, axis_index_groups=cores, tiled=True,
        )
        return mine, lax.ppermute(mine, "row", swap)

    code_rows = jnp.zeros((16, 128), bf16).at[0, :SLOTS].set(own_place.astype(bf16))
    mine, other = column_panel(jnp.concatenate([pairs.reshape(2 * BS, 2 * BS), code_rows], axis=0))
    codes_mine = mine[:, 2 * BS, :SLOTS].astype(jnp.int32)
    codes_other = other[:, 2 * BS, :SLOTS].astype(jnp.int32)
    is_even = core == 0
    codes_right = jnp.stack(
        [jnp.where(is_even, codes_mine, codes_other), jnp.where(is_even, codes_other, codes_mine)],
        axis=1,
    ).reshape(-1)

    scale = 1.5 / math.sqrt(BS * SLOTS * col_count / (block_count // row_count))
    depth = col_count * TILE
    core_word = core.astype(jnp.int32).reshape(1)
    params = pltpu.CompilerParams(vmem_limit_bytes=48 * 1024 * 1024)
    square, dense_left = pl.pallas_call(
        lambda *refs: first_kernel(scale, *refs),
        out_shape=(
            jax.ShapeDtypeStruct(pairs.shape, bf16),
            jax.ShapeDtypeStruct((TILE, depth), bf16),
        ),
        in_specs=[SMEM] * 4 + [VMEM] * 3,
        out_specs=(VMEM, VMEM),
        scratch_shapes=[pltpu.VMEM((depth, TILE), bf16), pltpu.VMEM((TILE, TILE), jnp.float32)],
        compiler_params=params,
    )(codes_left, codes_right, own_place, core_word, left, mine, other)

    mine, other = column_panel(square.reshape(2 * BS, 2 * BS))
    sign_next = pl.pallas_call(
        lambda *refs: second_kernel(scale, *refs),
        out_shape=jax.ShapeDtypeStruct(pairs.shape, bf16),
        in_specs=[SMEM] * 3 + [VMEM] * 4,
        out_specs=VMEM,
        scratch_shapes=[pltpu.VMEM((depth, TILE), bf16), pltpu.VMEM((TILE, TILE), jnp.float32)],
        compiler_params=params,
    )(codes_right, own_place, core_word, dense_left, mine, other, pairs)
    return (unpack(square)[None], unpack(sign_next)[None])


def solution(mesh):
    in_specs = (P("row", "col", None), P("row", "col"), P(), P("row", "col", None), P("row", "col"))
    out_specs = (P("row", "col", None), P("row", "col", None))
    return jax.shard_map(local, mesh=mesh, in_specs=in_specs, out_specs=out_specs, check_vma=False)
```

```python
import math

import jax
import jax.numpy as jnp
from jax import lax
from jax.experimental import pallas as pl
from jax.experimental.pallas import tpu as pltpu
from jax.sharding import PartitionSpec as P

BS = 64
SLOTS = 4
SIDE = 4
TILE = BS * SIDE
LANES = 2 * BS
VMEM = pl.BlockSpec(memory_space=pltpu.VMEM)
SMEM = pl.BlockSpec(memory_space=pltpu.SMEM)
ANY = pl.BlockSpec(memory_space=pl.ANY)
BF16 = jnp.bfloat16
F32 = jnp.float32
I32 = jnp.int32


def params(megabytes):
    return pltpu.CompilerParams(vmem_limit_bytes=megabytes * 1024 * 1024)


def cost(flops, megabytes):
    return pl.CostEstimate(flops=flops, bytes_accessed=megabytes * 1024 * 1024, transcendentals=0)


def pack(blocks):
    return blocks.reshape(2, 2, BS, BS).transpose(0, 2, 1, 3).reshape(2, BS, LANES)


def unpack(pairs):
    return pairs.reshape(2, BS, 2, BS).transpose(0, 2, 1, 3).reshape(SLOTS, BS * BS)


def swap_halves(x):
    return jnp.concatenate([x[:, BS:], x[:, :BS]], axis=1)


def place_pair(dense, row, column, pair, spots, fresh):
    lane = lax.broadcasted_iota(I32, (1, LANES), 1)
    low = jnp.where(lane < BS, 1.0, 0.0).astype(BF16)
    high = jnp.where(lane < BS, 0.0, 1.0).astype(BF16)
    swapped = swap_halves(pair)
    for slot, spot in enumerate(spots):
        half = spot & 1
        block = jnp.where(half == slot, pair, swapped) * jnp.where(half == 0, low, high)
        rows = pl.ds(pl.multiple_of(row + (spot >> 2) * BS, BS), BS)
        columns = pl.ds(pl.multiple_of(column + ((spot & 3) >> 1) * LANES, LANES), LANES)
        if fresh and slot == 0:
            dense[rows, columns] = block
        else:
            dense[rows, columns] = dense[rows, columns] + block


def payload_kernel(places_per, count, words, blocks, payload):
    shift = count.bit_length() - 1
    width = blocks.shape[-1]
    items = payload.shape[0] * places_per
    payload[:, :, :width] = blocks[...]
    lane = lax.broadcasted_iota(I32, (1, LANES), 1)
    base = jnp.zeros((1, LANES), I32)
    for slot in range(SLOTS):
        code = words[items + count + slot]
        spot = ((code >> shift) & (SIDE - 1)) * SIDE + (code & (SIDE - 1))
        base = jnp.where(lane == 1 + slot, spot, base)

    def body(j, carry):
        rows = []
        for k in range(places_per):
            task = words[j * places_per + k]
            safe = jnp.maximum(task, 0)
            block_row = words[items + (safe >> shift)] & (SIDE - 1)
            block_column = words[items + (safe & (count - 1))] & (SIDE - 1)
            spot = jnp.where(task < 0, -1, block_row * SIDE + block_column)
            rows.append(jnp.where(lane == 0, spot, base))
        payload[j, :, width:] = jnp.concatenate(rows, axis=0).astype(F32).astype(BF16)
        return carry

    lax.fori_loop(0, payload.shape[0], body, 0, unroll=4)


def left_kernel(codes, core, panel, dense, work, sems):
    copies = []
    for half in range(2):
        work[half] = jnp.zeros(work.shape[1:], work.dtype)

        def body(u, carry, half=half):
            t = 2 * u + (core[0] ^ half)
            for pair in range(2):
                at = t * SLOTS + 2 * pair
                spots = (codes[at], codes[at + 1])
                place_pair(work.at[half], 0, u * TILE, panel[t, pair], spots, pair == 0)
            return carry

        lax.fori_loop(0, panel.shape[0] // 2, body, 0, unroll=4)
        copies.append(pltpu.make_async_copy(work.at[half], dense.at[half], sems.at[half]))
        copies[half].start()
    for copy in copies:
        copy.wait()


def partial_product(codes, first_code, source, left, which, panel, right, left_half, sem):
    copy = pltpu.make_async_copy(left.at[which], left_half, sem)
    copy.start()
    right[...] = jnp.zeros_like(right)

    def body(e, carry):
        row = source(e) * TILE
        for pair in range(2):
            at = e * 2 * SLOTS + first_code + 2 * pair
            data = panel[e, pair * BS : (pair + 1) * BS, :]
            place_pair(right, row, 0, data, (codes[at], codes[at + 1]), pair == 0)
        return carry

    lax.fori_loop(0, panel.shape[0], body, 0, unroll=4)
    copy.wait()
    return jnp.dot(left_half[...], right[...], preferred_element_type=F32)


def source_of(flipped, chip):
    return (lambda e: e ^ (chip & 1)) if flipped else lambda e: e


def own_pairs(total, own):
    lane = lax.broadcasted_iota(I32, (BS, LANES), 1)
    pairs = []
    for pair in range(2):
        parts = []
        for slot in (2 * pair, 2 * pair + 1):
            spot = own[slot]
            rows = pl.ds(pl.multiple_of((spot // SIDE) * BS, BS), BS)
            columns = pl.ds(pl.multiple_of(((spot % SIDE) // 2) * LANES, LANES), LANES)
            block = total[rows, columns]
            parts.append(jnp.where(spot % 2 == slot % 2, block, pltpu.roll(block, BS, 1)))
        pairs.append(jnp.where(lane < BS, parts[0], parts[1]))
    return pairs


def first_half_kernel(flipped, codes, chip, left, panel, total, *scratch):
    source = source_of(flipped, chip[0])
    total[...] = partial_product(codes, 0, source, left, 0, panel, *scratch)


def finish(flipped, codes, chip, own, left, panel, before, total, *scratch):
    source = source_of(flipped, chip[0])
    total[...] = before[...] + partial_product(
        codes, SLOTS, source, left, 1, panel, *scratch
    )
    return own_pairs(total, own)


def square_kernel(scale, codes, chip, own, left, panel, before, square, codes_by_chip, *scratch):
    source = source_of(True, chip[0])

    def body(e, carry):
        for slot in range(2 * SLOTS):
            codes_by_chip[source(e) * 2 * SLOTS + slot] = codes[e * 2 * SLOTS + slot]
        return carry

    lax.fori_loop(0, panel.shape[0], body, 0)
    for pair, value in enumerate(finish(True, codes, chip, own, left, panel, before, *scratch)):
        square[pair] = (scale * value).astype(square.dtype)


def sign_kernel(scale, codes, chip, own, left, panel, before, matrix, sign_next, *scratch):
    for pair, value in enumerate(finish(False, codes, chip, own, left, panel, before, *scratch)):
        old = matrix[pair].astype(F32)
        sign_next[pair] = (1.5 * old - 0.5 * scale * value).astype(sign_next.dtype)


def local(matrix_blocks, block_codes, block_perm, grid_blocks, grid_tasks):
    col_count = lax.axis_size("col")
    row_count = lax.axis_size("row")
    chips = row_count // 2
    block_count = block_perm.shape[0]
    barrier = lax.optimization_barrier
    row = lax.axis_index("row")
    core_word = (row % 2).astype(I32).reshape(1)
    chip_word = (row // 2).astype(I32).reshape(1)
    own_codes = block_codes[0]
    own_place = (own_codes // block_count) % SIDE * SIDE + own_codes % SIDE

    def permute(x, mask):
        return lax.ppermute(x, "row", [(i, i ^ mask) for i in range(row_count)])

    cap = grid_tasks.shape[1] // col_count
    width = grid_blocks.shape[-1]
    words = jnp.concatenate([grid_tasks[0], block_perm, own_codes])
    payload = pl.pallas_call(
        lambda *refs: payload_kernel(cap, block_count, *refs),
        out_shape=jax.ShapeDtypeStruct((col_count, cap, width + LANES), BF16),
        in_specs=[SMEM, VMEM],
        out_specs=VMEM,
        compiler_params=params(8),
    )(words, grid_blocks[0].reshape(col_count, cap, width))
    received = lax.all_to_all(payload, "col", 0, 0, tiled=True)
    partner_place = permute(own_place, 1)
    codes_left = received[:, 0, width + 1 : width + 1 + SLOTS].astype(I32).reshape(-1)
    arrived_place = received[:, :, width].astype(I32).reshape(-1)
    items = received.reshape(-1, width + LANES)
    matches = (own_place[:, None] == arrived_place[None, :]).astype(BF16)
    grid_sum = jnp.dot(matches, items, preferred_element_type=F32)[:, :width]
    matrix = (matrix_blocks[0].astype(F32) + grid_sum).astype(BF16)
    pairs = barrier(pack(matrix))

    rows = pairs.reshape(2 * BS, LANES)
    panel = lax.all_to_all(
        jnp.broadcast_to(rows[None], (col_count,) + rows.shape), "col", 0, 0, tiled=True
    ).reshape((col_count,) + pairs.shape)
    chip_codes = jnp.concatenate([own_place, partner_place]).astype(BF16)
    code_rows = jnp.zeros((16, LANES), BF16).at[0, : 2 * SLOTS].set(chip_codes)
    tile = jnp.concatenate([rows, code_rows], axis=0)
    both = jnp.stack([tile, permute(tile, 2)])
    panel, both = barrier((panel, both))
    half_shape = (TILE, col_count // 2 * TILE)
    left = pl.pallas_call(
        left_kernel,
        out_shape=jax.ShapeDtypeStruct((10,) + half_shape, BF16),
        in_specs=[SMEM] * 2 + [VMEM],
        out_specs=ANY,
        scratch_shapes=[pltpu.VMEM((2,) + half_shape, BF16), pltpu.SemaphoreType.DMA((2,))],
        compiler_params=params(48),
        cost_estimate=cost(1 << 32, 8),
    )(codes_left, core_word, panel)
    lines = [[4 * z + k for z in range(row_count // 4)] for k in range(4)]
    mine = lax.all_to_all(
        jnp.broadcast_to(both[None], (row_count // 4,) + both.shape),
        "row", 0, 0, axis_index_groups=lines, tiled=True,
    ).reshape((chips,) + tile.shape)
    mine, left = barrier((mine, left))
    codes_right = mine[:, 2 * BS, : 2 * SLOTS].astype(I32).reshape(-1)
    other = permute(mine, 1)

    scale = 1.5 / math.sqrt(BS * SLOTS * col_count / (block_count // row_count))
    depth = col_count * TILE
    total_shape = jax.ShapeDtypeStruct((TILE, TILE), F32)
    tile_shape = jax.ShapeDtypeStruct(pairs.shape, BF16)
    work = [
        pltpu.VMEM((depth // 2, TILE), BF16),
        pltpu.VMEM((TILE, depth // 2), BF16),
        pltpu.SemaphoreType.DMA,
    ]
    settings = dict(
        compiler_params=params(48), cost_estimate=cost(2 * TILE * TILE * depth // 2, 6)
    )

    def first_half(flipped, codes, mine):
        return pl.pallas_call(
            lambda *refs: first_half_kernel(flipped, *refs),
            out_shape=total_shape,
            in_specs=[SMEM] * 2 + [ANY, VMEM],
            out_specs=VMEM,
            scratch_shapes=work,
            **settings,
        )(codes, chip_word, left, mine)

    before = first_half(True, codes_right, mine)
    square, codes_by_chip = pl.pallas_call(
        lambda *refs: square_kernel(scale, *refs),
        out_shape=(tile_shape, jax.ShapeDtypeStruct(codes_right.shape, I32)),
        in_specs=[SMEM] * 3 + [ANY] + [VMEM] * 2,
        out_specs=(VMEM, SMEM),
        scratch_shapes=[pltpu.VMEM((TILE, TILE), F32)] + work,
        **settings,
    )(codes_right, chip_word, own_place, left, other, before)

    cores = [[2 * chip + one for chip in range(chips)] for one in range(2)]
    rows = square.reshape(2 * BS, LANES)
    mine = lax.all_to_all(
        jnp.broadcast_to(rows[None], (chips,) + rows.shape),
        "row", 0, 0, axis_index_groups=cores, tiled=True,
    )
    square_out = unpack(square)[None]
    mine, square_out = barrier((mine, square_out))
    other = permute(mine, 1)
    before = first_half(False, codes_by_chip, mine)
    sign_next = pl.pallas_call(
        lambda *refs: sign_kernel(scale, *refs),
        out_shape=tile_shape,
        in_specs=[SMEM] * 3 + [ANY] + [VMEM] * 3,
        out_specs=VMEM,
        scratch_shapes=[pltpu.VMEM((TILE, TILE), F32)] + work,
        **settings,
    )(codes_by_chip, chip_word, own_place, left, other, before, pairs)
    return (square_out, unpack(sign_next)[None])


def solution(mesh):
    in_specs = (P("row", "col", None), P("row", "col"), P(), P("row", "col", None), P("row", "col"))
    out_specs = (P("row", "col", None), P("row", "col", None))
    return jax.shard_map(local, mesh=mesh, in_specs=in_specs, out_specs=out_specs, check_vma=False)
```

```python
import math

import jax
import jax.numpy as jnp
from jax import lax
from jax.experimental import pallas as pl
from jax.experimental.pallas import tpu as pltpu
from jax.sharding import PartitionSpec as P

BS = 64
SLOTS = 4
SIDE = 4
TILE = BS * SIDE
LANES = 2 * BS
VMEM = pl.BlockSpec(memory_space=pltpu.VMEM)
SMEM = pl.BlockSpec(memory_space=pltpu.SMEM)
ANY = pl.BlockSpec(memory_space=pl.ANY)
BF16 = jnp.bfloat16
F32 = jnp.float32
I32 = jnp.int32


def params(megabytes):
    return pltpu.CompilerParams(vmem_limit_bytes=megabytes * 1024 * 1024)


def cost(flops, megabytes):
    return pl.CostEstimate(flops=flops, bytes_accessed=megabytes * 1024 * 1024, transcendentals=0)


def pack(blocks):
    return blocks.reshape(2, 2, BS, BS).transpose(0, 2, 1, 3).reshape(2, BS, LANES)


def unpack(pairs):
    return pairs.reshape(2, BS, 2, BS).transpose(0, 2, 1, 3).reshape(SLOTS, BS * BS)


def swap_halves(x):
    return jnp.concatenate([x[:, BS:], x[:, :BS]], axis=1)


def place_pair(dense, row, column, pair, spots, fresh):
    lane = lax.broadcasted_iota(I32, (1, LANES), 1)
    low = jnp.where(lane < BS, 1.0, 0.0).astype(BF16)
    high = jnp.where(lane < BS, 0.0, 1.0).astype(BF16)
    swapped = swap_halves(pair)
    for slot, spot in enumerate(spots):
        half = spot & 1
        block = jnp.where(half == slot, pair, swapped) * jnp.where(half == 0, low, high)
        rows = pl.ds(pl.multiple_of(row + (spot >> 2) * BS, BS), BS)
        columns = pl.ds(pl.multiple_of(column + ((spot & 3) >> 1) * LANES, LANES), LANES)
        if fresh and slot == 0:
            dense[rows, columns] = block
        else:
            dense[rows, columns] = dense[rows, columns] + block


def payload_kernel(places_per, count, words, blocks, payload):
    shift = count.bit_length() - 1
    width = blocks.shape[-1]
    items = payload.shape[0] * places_per
    for first in range(0, blocks.shape[0], 16):
        owners = pl.ds(first // places_per, 16 // places_per)
        payload[owners, :, :width] = blocks[first : first + 16].reshape(
            16 // places_per, places_per, width
        )
    lane = lax.broadcasted_iota(I32, (1, LANES), 1)
    base = jnp.zeros((1, LANES), I32)
    for slot in range(SLOTS):
        code = words[items + count + slot]
        spot = ((code >> shift) & (SIDE - 1)) * SIDE + (code & (SIDE - 1))
        base = jnp.where(lane == 1 + slot, spot, base)

    def body(j, carry):
        rows = []
        for k in range(places_per):
            task = words[j * places_per + k]
            safe = jnp.maximum(task, 0)
            block_row = words[items + (safe >> shift)] & (SIDE - 1)
            block_column = words[items + (safe & (count - 1))] & (SIDE - 1)
            spot = jnp.where(task < 0, -1, block_row * SIDE + block_column)
            rows.append(jnp.where(lane == 0, spot, base))
        payload[j, :, width:] = jnp.concatenate(rows, axis=0).astype(F32).astype(BF16)
        return carry

    lax.fori_loop(0, payload.shape[0], body, 0, unroll=8)


def spread_kernel(tile, copies, sems):
    sends = [
        pltpu.make_async_copy(tile, copies.at[k], sems.at[k]) for k in range(copies.shape[0])
    ]
    for send in sends:
        send.start()
    for send in sends:
        send.wait()


def spread(tile, count):
    return pl.pallas_call(
        spread_kernel,
        out_shape=jax.ShapeDtypeStruct((count,) + tile.shape, tile.dtype),
        in_specs=[VMEM],
        out_specs=ANY,
        scratch_shapes=[pltpu.SemaphoreType.DMA((count,))],
        compiler_params=params(8),
    )(tile)


def left_kernel(codes, partner_codes, place, panel, far, near, work, sem):
    core = place[0]
    count = panel.shape[0] // 4

    def fill(dense, first):
        dense[...] = jnp.zeros_like(dense)

        def body(v, carry):
            t = 2 * (first + v) + core
            for first_row, entry, source in ((0, t, codes), (TILE, t ^ 1, partner_codes)):
                for pair in range(2):
                    at = t * SLOTS + 2 * pair
                    spots = (source[at], source[at + 1])
                    place_pair(dense, first_row, v * TILE, panel[entry, pair], spots, pair == 0)
            return carry

        lax.fori_loop(0, count, body, 0, unroll=4)

    fill(work, count)
    copy = pltpu.make_async_copy(work, far.at[0], sem)
    copy.start()
    fill(near, 0)
    copy.wait()


def mirror(e):
    return (e & 5) | ((e & 2) << 2) | ((e & 8) >> 2)


def orders(doubled, chip):
    if doubled:
        return (lambda e: chip ^ mirror(e)), (lambda e: e)
    return (lambda e: e), (lambda e: mirror(e ^ chip))


def fill_right(doubled, codes, chip, panels, right):
    right[...] = jnp.zeros_like(right)
    slot, entry = orders(doubled, chip)
    first = 0
    for k, panel in enumerate(panels):

        def body(e, carry, first=first, panel=panel, codes=codes[k]):
            row = slot(first + e) * TILE
            for pair in range(2):
                at = (entry(first + e) - first) * SLOTS + 2 * pair
                data = panel[e, pair * BS : (pair + 1) * BS, :]
                place_pair(right, row, 0, data, (codes[at], codes[at + 1]), pair == 0)
            return carry

        lax.fori_loop(0, panel.shape[0], body, 0, unroll=4)
        first += panel.shape[0]


def own_pairs(total, first_row, own):
    lane = lax.broadcasted_iota(I32, (BS, LANES), 1)
    pairs = []
    for pair in range(2):
        parts = []
        for slot in (2 * pair, 2 * pair + 1):
            spot = own[slot]
            rows = pl.ds(pl.multiple_of(first_row + (spot >> 2) * BS, BS), BS)
            columns = pl.ds(pl.multiple_of(((spot & 3) >> 1) * LANES, LANES), LANES)
            block = total[rows, columns]
            parts.append(jnp.where(spot % 2 == slot % 2, block, pltpu.roll(block, BS, 1)))
        pairs.append(jnp.where(lane < BS, parts[0], parts[1]))
    return pairs


def product_kernel(doubled, count, place, own, theirs, far, near, *refs):
    codes, panels = refs[:count], refs[count : 2 * count]
    kept, sent, total, right, left, sem = refs[2 * count :]
    copy = pltpu.make_async_copy(far.at[0], left, sem)
    copy.start()
    fill_right(doubled, codes, place[1], panels, right)
    depth = near.shape[1]
    total[...] = jnp.dot(near[...], right[:depth], preferred_element_type=F32)
    copy.wait()
    total[...] += jnp.dot(left[...], right[depth:], preferred_element_type=F32)
    for out, first_row, spots in ((sent, TILE, theirs), (kept, 0, own)):
        for pair, value in enumerate(own_pairs(total, first_row, spots)):
            out[pair * BS : (pair + 1) * BS] = value


def square_kernel(scale, kept, received, square, copies, sems):
    square[...] = (scale * (kept[...] + received[...])).astype(square.dtype)
    spread_kernel(square, copies, sems)


def local(matrix_blocks, block_codes, block_perm, grid_blocks, grid_tasks):
    col_count = lax.axis_size("col")
    row_count = lax.axis_size("row")
    block_count = block_perm.shape[0]
    barrier = lax.optimization_barrier
    row = lax.axis_index("row")
    place = jnp.stack([row % 2, row // 2]).astype(I32)
    own_codes = block_codes[0]
    own_place = (own_codes // block_count) % SIDE * SIDE + own_codes % SIDE

    def permute(x, mask):
        return lax.ppermute(x, "row", [(i, i ^ mask) for i in range(row_count)])

    cap = grid_tasks.shape[1] // col_count
    width = grid_blocks.shape[-1]
    words = jnp.concatenate([grid_tasks[0], block_perm, own_codes])
    payload = pl.pallas_call(
        lambda *refs: payload_kernel(cap, block_count, *refs),
        out_shape=jax.ShapeDtypeStruct((col_count, cap, width + LANES), BF16),
        in_specs=[SMEM, VMEM],
        out_specs=VMEM,
        compiler_params=params(8),
    )(words, grid_blocks[0])
    received = lax.all_to_all(payload, "col", 0, 0, tiled=True)
    received, theirs = barrier((received, permute(own_place, 1)))
    codes_left = received[:, 0, width + 1 : width + 1 + SLOTS].astype(I32).reshape(-1)
    arrived_place = received[:, :, width].astype(I32).reshape(-1)
    items = received.reshape(-1, width + LANES)
    matches = (own_place[:, None] == arrived_place[None, :]).astype(BF16)
    grid_sum = jnp.dot(matches, items, preferred_element_type=F32)[:, :width]
    matrix = (matrix_blocks[0].astype(F32) + grid_sum).astype(BF16)
    pairs = barrier(pack(matrix))

    moves = []
    for r in range(row_count):
        for c in range(col_count):
            moves_on = (r ^ c) & 1
            target = (r ^ moves_on) * col_count + (c ^ moves_on)
            moves.append((r * col_count + c, target))
    rows = pairs.reshape(2 * BS, LANES)
    code_rows = jnp.zeros((8, LANES), BF16).at[0, :SLOTS].set(own_place.astype(BF16))
    tile = jnp.concatenate([rows, code_rows], axis=0)
    moved, across = barrier((lax.ppermute(rows, ("row", "col"), moves), permute(tile, 2)))

    panel = lax.all_to_all(spread(moved, col_count), "col", 0, 0, tiled=True).reshape(
        (col_count,) + pairs.shape
    )

    scale = 1.5 / math.sqrt(BS * SLOTS * col_count / (block_count // row_count))
    depth = col_count // 4 * TILE
    half_shape = (2 * TILE, depth)
    tile_shape = jax.ShapeDtypeStruct(rows.shape, F32)
    settings = dict(compiler_params=params(48), cost_estimate=cost(8 * TILE * TILE * depth, 6))
    gathered = jnp.stack([tile, across])
    for mask in (16, 8):
        gathered = jnp.concatenate([gathered, permute(gathered, mask)], axis=0)
    codes_left, gathered = barrier((codes_left, gathered))
    partner_codes = permute(codes_left, 1)
    far, near = pl.pallas_call(
        left_kernel,
        out_shape=(
            jax.ShapeDtypeStruct((10,) + half_shape, BF16),
            jax.ShapeDtypeStruct(half_shape, BF16),
        ),
        in_specs=[SMEM] * 3 + [VMEM],
        out_specs=(ANY, VMEM),
        scratch_shapes=[pltpu.VMEM(half_shape, BF16), pltpu.SemaphoreType.DMA],
        **settings,
    )(codes_left, partner_codes, place, panel)

    last, far, near = barrier((permute(gathered, 4), far, near))
    panels = [gathered, last]
    codes = [part[:, 2 * BS, :SLOTS].astype(I32).reshape(-1) for part in panels]

    def product(doubled, codes, panels):
        count = len(panels)
        kept, sent = pl.pallas_call(
            lambda *refs: product_kernel(doubled, count, *refs),
            out_shape=(tile_shape, tile_shape),
            in_specs=[SMEM] * 3 + [ANY, VMEM] + [SMEM] * count + [VMEM] * count,
            out_specs=(VMEM, VMEM),
            scratch_shapes=[
                pltpu.VMEM((2 * TILE, TILE), F32),
                pltpu.VMEM((2 * depth, TILE), BF16),
                pltpu.VMEM(half_shape, BF16),
                pltpu.SemaphoreType.DMA,
            ],
            **settings,
        )(place, own_place, theirs, far, near, *codes, *panels)
        return kept, permute(sent, 1)

    kept, received = product(True, codes, panels)
    chips = row_count // 2
    square, copies = pl.pallas_call(
        lambda *refs: square_kernel(scale, *refs),
        out_shape=(
            jax.ShapeDtypeStruct(rows.shape, BF16),
            jax.ShapeDtypeStruct((chips,) + rows.shape, BF16),
        ),
        in_specs=[VMEM] * 2,
        out_specs=(VMEM, ANY),
        scratch_shapes=[pltpu.SemaphoreType.DMA((chips,))],
        compiler_params=params(8),
    )(kept, received)
    cores = [[2 * chip + one for chip in range(chips)] for one in range(2)]
    tiles = lax.all_to_all(copies, "row", 0, 0, axis_index_groups=cores, tiled=True)
    square_out = unpack(square.reshape(pairs.shape))[None]
    tiles, square_out = barrier((tiles, square_out))
    kept, received = product(False, [jnp.concatenate(codes)], [tiles])
    second = unpack((kept + received).reshape(pairs.shape))
    sign_next = (1.5 * matrix.astype(F32) - 0.5 * scale * second).astype(BF16)
    return (square_out, sign_next[None])


def solution(mesh):
    in_specs = (P("row", "col", None), P("row", "col"), P(), P("row", "col", None), P("row", "col"))
    out_specs = (P("row", "col", None), P("row", "col", None))
    return jax.shard_map(local, mesh=mesh, in_specs=in_specs, out_specs=out_specs, check_vma=False)
```

```python
import math

import jax
import jax.numpy as jnp
from jax import lax
from jax.experimental import pallas as pl
from jax.experimental.pallas import tpu as pltpu
from jax.sharding import PartitionSpec as P

BS = 64
SLOTS = 4
SIDE = 4
TILE = BS * SIDE
LANES = 2 * BS
VMEM = pl.BlockSpec(memory_space=pltpu.VMEM)
SMEM = pl.BlockSpec(memory_space=pltpu.SMEM)
ANY = pl.BlockSpec(memory_space=pl.ANY)
BF16 = jnp.bfloat16
F32 = jnp.float32
I32 = jnp.int32


def params(megabytes):
    return pltpu.CompilerParams(vmem_limit_bytes=megabytes * 1024 * 1024)


def cost(flops, megabytes):
    return pl.CostEstimate(flops=flops, bytes_accessed=megabytes * 1024 * 1024, transcendentals=0)


def pack(blocks):
    return blocks.reshape(2, 2, BS, BS).transpose(0, 2, 1, 3).reshape(2, BS, LANES)


def unpack(pairs):
    return pairs.reshape(2, BS, 2, BS).transpose(0, 2, 1, 3).reshape(SLOTS, BS * BS)


def swap_halves(x):
    return jnp.concatenate([x[:, BS:], x[:, :BS]], axis=1)


def place_pair(dense, row, column, pair, spots, fresh):
    lane = lax.broadcasted_iota(I32, (1, LANES), 1)
    low = jnp.where(lane < BS, 1.0, 0.0).astype(BF16)
    high = jnp.where(lane < BS, 0.0, 1.0).astype(BF16)
    swapped = swap_halves(pair)
    for slot, spot in enumerate(spots):
        half = spot & 1
        block = jnp.where(half == slot, pair, swapped) * jnp.where(half == 0, low, high)
        rows = pl.ds(pl.multiple_of(row + (spot >> 2) * BS, BS), BS)
        columns = pl.ds(pl.multiple_of(column + ((spot & 3) >> 1) * LANES, LANES), LANES)
        if fresh and slot == 0:
            dense[rows, columns] = block
        else:
            dense[rows, columns] = dense[rows, columns] + block


def tail_kernel(places_per, count, words, tail):
    shift = count.bit_length() - 1
    items = tail.shape[0] * places_per
    lane = lax.broadcasted_iota(I32, (1, LANES), 1)
    base = jnp.zeros((1, LANES), I32)
    for slot in range(SLOTS):
        code = words[items + count + slot]
        spot = ((code >> shift) & (SIDE - 1)) * SIDE + (code & (SIDE - 1))
        base = jnp.where(lane == 1 + slot, spot, base)

    def body(j, carry):
        rows = []
        for k in range(places_per):
            task = words[j * places_per + k]
            safe = jnp.maximum(task, 0)
            block_row = words[items + (safe >> shift)] & (SIDE - 1)
            block_column = words[items + (safe & (count - 1))] & (SIDE - 1)
            spot = jnp.where(task < 0, -1, block_row * SIDE + block_column)
            rows.append(jnp.where(lane == 0, spot, base))
        tail[j] = jnp.concatenate(rows, axis=0).astype(F32).astype(BF16)
        return carry

    lax.fori_loop(0, tail.shape[0], body, 0, unroll=8)


def payload_kernel(places_per, tail, blocks, payload):
    width = blocks.shape[-1]
    for first in range(0, blocks.shape[0], 16):
        owners = pl.ds(first // places_per, 16 // places_per)
        payload[owners, :, :width] = blocks[first : first + 16].reshape(
            16 // places_per, places_per, width
        )
    payload[:, :, width:] = tail[...]


def combine_kernel(own, received, before, matrix):
    width = before.shape[-1]
    per, cap = 16 // received.shape[1], received.shape[1]
    lane = lax.broadcasted_iota(I32, (1, 8), 1)
    spots = jnp.full((1, 8), -2, I32)
    for slot in range(SLOTS):
        spots = jnp.where(lane == slot, own[slot], spots)
    spots = spots.astype(F32)
    total = jnp.zeros((8, width), F32)
    parts, marks = [], []
    for first in range(0, received.shape[0], per):
        part = received[first : first + per].reshape(per * cap, received.shape[2])
        parts.append(part[:, :width])
        place = part[:, width : width + LANES].astype(F32)[:, :1]
        marks.append(jnp.where(place == spots, 1.0, 0.0).astype(BF16))
    total = lax.dot_general(
        jnp.concatenate(marks, axis=0),
        jnp.concatenate(parts, axis=0),
        (((0,), (0,)), ((), ())),
        preferred_element_type=F32,
    )
    matrix[...] = (before[...].astype(F32) + total[:SLOTS]).astype(BF16)


def spread_kernel(tile, copies, sems):
    sends = [
        pltpu.make_async_copy(tile, copies.at[k], sems.at[k]) for k in range(copies.shape[0])
    ]
    for send in sends:
        send.start()
    for send in sends:
        send.wait()


def spread(tile, count):
    return pl.pallas_call(
        spread_kernel,
        out_shape=jax.ShapeDtypeStruct((count,) + tile.shape, tile.dtype),
        in_specs=[VMEM],
        out_specs=ANY,
        scratch_shapes=[pltpu.SemaphoreType.DMA((count,))],
        compiler_params=params(8),
    )(tile)


def left_kernel(codes, partner_codes, place, panel, far, near, work, sem):
    core = place[0]
    count = panel.shape[0] // 4

    def fill(dense, first):
        dense[...] = jnp.zeros_like(dense)

        def body(v, carry):
            t = 2 * (first + v) + core
            for first_row, entry, source in ((0, t, codes), (TILE, t ^ 1, partner_codes)):
                for pair in range(2):
                    at = t * SLOTS + 2 * pair
                    spots = (source[at], source[at + 1])
                    place_pair(dense, first_row, v * TILE, panel[entry, pair], spots, pair == 0)
            return carry

        lax.fori_loop(0, count, body, 0, unroll=4)

    fill(work, count)
    copy = pltpu.make_async_copy(work, far.at[0], sem)
    copy.start()
    fill(near, 0)
    copy.wait()


def mirror(e):
    return (e & 5) | ((e & 2) << 2) | ((e & 8) >> 2)


def orders(doubled, chip):
    if doubled:
        return (lambda e: chip ^ mirror(e)), (lambda e: e)
    return (lambda e: e), (lambda e: mirror(e ^ chip))


def fill_right(doubled, codes, chip, panels, right):
    right[...] = jnp.zeros_like(right)
    slot, entry = orders(doubled, chip)
    first = 0
    for k, panel in enumerate(panels):

        def body(e, carry, first=first, panel=panel, codes=codes[k]):
            row = slot(first + e) * TILE
            for pair in range(2):
                at = (entry(first + e) - first) * SLOTS + 2 * pair
                data = panel[e, pair * BS : (pair + 1) * BS, :]
                place_pair(right, row, 0, data, (codes[at], codes[at + 1]), pair == 0)
            return carry

        lax.fori_loop(0, panel.shape[0], body, 0, unroll=4)
        first += panel.shape[0]


def own_pairs(total, first_row, own):
    lane = lax.broadcasted_iota(I32, (BS, LANES), 1)
    pairs = []
    for pair in range(2):
        parts = []
        for slot in (2 * pair, 2 * pair + 1):
            spot = own[slot]
            rows = pl.ds(pl.multiple_of(first_row + (spot >> 2) * BS, BS), BS)
            columns = pl.ds(pl.multiple_of(((spot & 3) >> 1) * LANES, LANES), LANES)
            block = total[rows, columns]
            parts.append(jnp.where(spot % 2 == slot % 2, block, pltpu.roll(block, BS, 1)))
        pairs.append(jnp.where(lane < BS, parts[0], parts[1]))
    return pairs


def product_kernel(doubled, count, place, own, theirs, far, near, *refs):
    codes, panels = refs[:count], refs[count : 2 * count]
    kept, sent, total, right, left, sem = refs[2 * count :]
    copy = pltpu.make_async_copy(far.at[0], left, sem)
    copy.start()
    fill_right(doubled, codes, place[1], panels, right)
    depth = near.shape[1]
    total[...] = jnp.dot(near[...], right[:depth], preferred_element_type=F32)
    copy.wait()
    total[...] += jnp.dot(left[...], right[depth:], preferred_element_type=F32)
    for out, first_row, spots in ((sent, TILE, theirs), (kept, 0, own)):
        for pair, value in enumerate(own_pairs(total, first_row, spots)):
            out[pair * BS : (pair + 1) * BS] = value


def square_kernel(scale, kept, received, square, copies, sems):
    square[...] = (scale * (kept[...] + received[...])).astype(square.dtype)
    spread_kernel(square, copies, sems)


def local(matrix_blocks, block_codes, block_perm, grid_blocks, grid_tasks):
    col_count = lax.axis_size("col")
    row_count = lax.axis_size("row")
    block_count = block_perm.shape[0]
    barrier = lax.optimization_barrier
    row = lax.axis_index("row")
    place = jnp.stack([row % 2, row // 2]).astype(I32)
    own_codes = block_codes[0]
    own_place = (own_codes // block_count) % SIDE * SIDE + own_codes % SIDE

    def permute(x, mask):
        return lax.ppermute(x, "row", [(i, i ^ mask) for i in range(row_count)])

    cap = grid_tasks.shape[1] // col_count
    width = grid_blocks.shape[-1]
    words = jnp.concatenate([grid_tasks[0], block_perm, own_codes])
    tail = pl.pallas_call(
        lambda *refs: tail_kernel(cap, block_count, *refs),
        out_shape=jax.ShapeDtypeStruct((col_count, cap, LANES), BF16),
        in_specs=[SMEM],
        out_specs=VMEM,
        compiler_params=params(8),
    )(words)
    payload = pl.pallas_call(
        lambda *refs: payload_kernel(cap, *refs),
        out_shape=jax.ShapeDtypeStruct((col_count, cap, width + LANES), BF16),
        in_specs=[VMEM] * 2,
        out_specs=VMEM,
        compiler_params=params(8),
    )(tail, grid_blocks[0])
    received = lax.all_to_all(payload, "col", 0, 0, tiled=True)
    received, theirs, stored = barrier(
        (received, permute(own_place, 1), matrix_blocks[0].astype(F32))
    )
    codes_left = received[:, 0, width + 1 : width + 1 + SLOTS].astype(I32).reshape(-1)
    matrix = pl.pallas_call(
        combine_kernel,
        out_shape=jax.ShapeDtypeStruct((SLOTS, width), BF16),
        in_specs=[SMEM] + [VMEM] * 2,
        out_specs=VMEM,
        compiler_params=params(8),
    )(own_place, received, stored)
    pairs = barrier(pack(matrix))

    moves = []
    for r in range(row_count):
        for c in range(col_count):
            moves_on = (r ^ c) & 1
            target = (r ^ moves_on) * col_count + (c ^ moves_on)
            moves.append((r * col_count + c, target))
    rows = pairs.reshape(2 * BS, LANES)
    code_rows = jnp.zeros((8, LANES), BF16).at[0, :SLOTS].set(own_place.astype(BF16))
    tile = jnp.concatenate([rows, code_rows], axis=0)
    moved, across = barrier((lax.ppermute(rows, ("row", "col"), moves), permute(tile, 2)))

    panel = lax.all_to_all(spread(moved, col_count), "col", 0, 0, tiled=True).reshape(
        (col_count,) + pairs.shape
    )

    scale = 1.5 / math.sqrt(BS * SLOTS * col_count / (block_count // row_count))
    depth = col_count // 4 * TILE
    half_shape = (2 * TILE, depth)
    tile_shape = jax.ShapeDtypeStruct(rows.shape, F32)
    settings = dict(compiler_params=params(48), cost_estimate=cost(8 * TILE * TILE * depth, 6))
    gathered = jnp.stack([tile, across])
    for mask in (16, 8):
        gathered = jnp.concatenate([gathered, permute(gathered, mask)], axis=0)
    codes_left, gathered = barrier((codes_left, gathered))
    partner_codes = permute(codes_left, 1)
    far, near = pl.pallas_call(
        left_kernel,
        out_shape=(
            jax.ShapeDtypeStruct((10,) + half_shape, BF16),
            jax.ShapeDtypeStruct(half_shape, BF16),
        ),
        in_specs=[SMEM] * 3 + [VMEM],
        out_specs=(ANY, VMEM),
        scratch_shapes=[pltpu.VMEM(half_shape, BF16), pltpu.SemaphoreType.DMA],
        **settings,
    )(codes_left, partner_codes, place, panel)

    last, far, near = barrier((permute(gathered, 4), far, near))
    panels = [gathered, last]
    codes = [part[:, 2 * BS, :SLOTS].astype(I32).reshape(-1) for part in panels]

    def product(doubled, codes, panels):
        count = len(panels)
        kept, sent = pl.pallas_call(
            lambda *refs: product_kernel(doubled, count, *refs),
            out_shape=(tile_shape, tile_shape),
            in_specs=[SMEM] * 3 + [ANY, VMEM] + [SMEM] * count + [VMEM] * count,
            out_specs=(VMEM, VMEM),
            scratch_shapes=[
                pltpu.VMEM((2 * TILE, TILE), F32),
                pltpu.VMEM((2 * depth, TILE), BF16),
                pltpu.VMEM(half_shape, BF16),
                pltpu.SemaphoreType.DMA,
            ],
            **settings,
        )(place, own_place, theirs, far, near, *codes, *panels)
        return kept, permute(sent, 1)

    kept, received = product(True, codes, panels)
    chips = row_count // 2
    square, copies = pl.pallas_call(
        lambda *refs: square_kernel(scale, *refs),
        out_shape=(
            jax.ShapeDtypeStruct(rows.shape, BF16),
            jax.ShapeDtypeStruct((chips,) + rows.shape, BF16),
        ),
        in_specs=[VMEM] * 2,
        out_specs=(VMEM, ANY),
        scratch_shapes=[pltpu.SemaphoreType.DMA((chips,))],
        compiler_params=params(8),
    )(kept, received)
    cores = [[2 * chip + one for chip in range(chips)] for one in range(2)]
    tiles = lax.all_to_all(copies, "row", 0, 0, axis_index_groups=cores, tiled=True)
    square_out = unpack(square.reshape(pairs.shape))[None]
    tiles, square_out = barrier((tiles, square_out))
    kept, received = product(False, [jnp.concatenate(codes)], [tiles])
    second = unpack((kept + received).reshape(pairs.shape))
    sign_next = (1.5 * matrix.astype(F32) - 0.5 * scale * second).astype(BF16)
    return (square_out, sign_next[None])


def solution(mesh):
    in_specs = (P("row", "col", None), P("row", "col"), P(), P("row", "col", None), P("row", "col"))
    out_specs = (P("row", "col", None), P("row", "col", None))
    return jax.shard_map(local, mesh=mesh, in_specs=in_specs, out_specs=out_specs, check_vma=False)
```
